32 devices in a mesh: dp: 4 (over y, x), space: 8 (over z, core).
Axes of the slice: x: 2, y: 2, z: 4, core: 2. Of those that a mesh axis runs over, the one named last changes fastest.
Arguments:
- features: bfloat16 [4, 128, 128, 256], P('dp', 'space'), may hold values from -6 to 6
- heights: float32 [4, 128, 128], P('dp', 'space'), may hold values from 0.02 to 2
- cotangent: bfloat16 [4, 128, 128, 256], P('dp', 'space'), may hold values from -6 to 6
- weight_first: bfloat16 [3, 3, 256, 256], replicated, may hold values from -0.125 to 0.125
- weight_second: bfloat16 [3, 3, 256, 256], replicated, may hold values from -0.125 to 0.125
- shade_embed: bfloat16 [256], replicated, may hold values from -4 to 4
Outputs:
- grad_features: bfloat16 [4, 128, 128, 256], P('dp', 'space')
- grad_first: float32 [3, 3, 256, 256], replicated
- grad_second: float32 [3, 3, 256, 256], replicated
- grad_embed: float32 [256], replicated
The draws below stay inside these ranges and needn't reach their ends.
All inputs are finite; a program needn't handle non-finite values.
Results may differ from the reference program's by a relative error of at most 0.012.
Values may be sent and summed in bfloat16 or wider, within the bound.
A program may use at most 64 MiB of HBM per device.

```python
import math
import jax
import jax.numpy as jnp
from jax import lax

C = 256
COLS = 128
ROWS = 128
IMGS = 4
PIXELS = 65536


def steps_of(rng, shape, split, smallest, top_value):
    loudness, own = 1.0, jax.random.fold_in(rng, 6)
    for axis_at, parts in split:
        steps = jnp.exp(jax.random.uniform(jax.random.fold_in(own, axis_at), (parts,), jnp.float32, smallest / len(split), top_value / len(split)))
        loudness = loudness * jnp.repeat(steps, shape[axis_at] // parts).reshape([-1 if axis == axis_at else 1 for axis in range(len(shape))])
    return loudness


def noise(stream_key, dims, width, limit, shards=(), kind=jnp.bfloat16):
    values = width * jax.random.normal(stream_key, dims, jnp.float32)
    if shards:
        values = values * steps_of(stream_key, dims, shards, -0.22, 0.18)
    return jnp.clip(values, -limit, limit).astype(kind)


def setup_inputs(seed: int = 0) -> dict:
    splits = jax.random.split(jax.random.key(seed), 7)
    return {
        "features": noise(splits[0], (IMGS, ROWS, COLS, C), 1.0, 6.0, ((0, 4), (1, 8))),
        "heights": jnp.clip(jnp.exp(math.log(2.0) - 4.6051702 * jax.random.uniform(splits[1], (IMGS, ROWS, COLS), jnp.float32) ** steps_of(splits[1], (IMGS, ROWS, COLS), ((0, 4), (1, 8)), -0.2, 0.2)), 0.02, 2.0),
        "cotangent": noise(splits[2], (IMGS, ROWS, COLS, C), 1.0, 6.0, ((0, 4), (1, 8))),
        "weight_first": noise(splits[3], (3, 3, C, C), (9 * C) ** -0.5, 0.125),
        "weight_second": noise(splits[4], (3, 3, C, C), (9 * C) ** -0.5, 0.125),
        "shade_embed": noise(splits[5], (C,), 1.0, 4.0),
    }


def convolve(padded, kernel):
    return lax.conv_general_dilated(padded, kernel, (1, 1), ((0, 0), (1, 1)), dimension_numbers=('NHWC', 'HWIO', 'NHWC'), preferred_element_type=jnp.float32)

def reversed_kernel(kernel):
    return jnp.transpose(jnp.flip(kernel, (0, 1)), (0, 1, 3, 2))

def pad_rows(values):
    return jnp.pad(values, ((0, 0), (1, 1), (0, 0), (0, 0)))

def silu_slope(values):
    sigma = jax.nn.sigmoid(values)
    return sigma * (1.0 + values * (1.0 - sigma))

def kernel_grad(padded, gradient):
    channels = gradient.shape[-1]
    row_count = gradient.shape[1]
    col_count = gradient.shape[2]
    widened = jnp.pad(padded, ((0, 0), (0, 0), (1, 1), (0, 0)))
    flat_grad = gradient.reshape(-1, channels)
    stacked = []
    for offset_row in range(3):
        line = []
        for offset_col in range(3):
            window = widened[:, offset_row:offset_row + row_count, offset_col:offset_col + col_count, :].reshape(-1, channels)
            line.append(jnp.dot(window.T, flat_grad, preferred_element_type=jnp.float32))
        stacked.append(jnp.stack(line))
    return jnp.stack(stacked)

def reference(features, heights, cotangent, weight_first, weight_second, shade_embed):
    decline = 2.0 / ROWS
    position = jnp.arange(ROWS).astype(jnp.float32)
    lifted = heights + decline * position[None, :, None]
    running = lax.cummax(lifted, axis=1)
    earlier_max = jnp.concatenate([jnp.zeros_like(running[:, :1, :]), running[:, :-1, :]], axis=1)
    shading = jnp.maximum(earlier_max - lifted, 0.0)
    scaling = 1.0 / math.sqrt(PIXELS)
    back_second = reversed_kernel(weight_second)
    back_first = reversed_kernel(weight_first)
    embed_wide = shade_embed.astype(jnp.float32)

    def per_image(totals, inputs):
        feature_one, shade_one, cot_one = inputs
        mixed = (feature_one.astype(jnp.float32) + shade_one[:, :, None] * embed_wide).astype(jnp.bfloat16)[None]
        padded_in = pad_rows(mixed)
        hidden_pre = convolve(padded_in, weight_first)
        active = jax.nn.silu(hidden_pre).astype(jnp.bfloat16)
        cot_batch = cot_one[None]
        back_act = convolve(pad_rows(cot_batch), back_second)
        back_hidden = (back_act * silu_slope(hidden_pre)).astype(jnp.bfloat16)
        back_input = convolve(pad_rows(back_hidden), back_first)
        grad_feature = (cot_batch.astype(jnp.float32) + back_input).astype(jnp.bfloat16)[0]
        first_term = kernel_grad(padded_in, back_hidden)
        second_term = kernel_grad(pad_rows(active), cot_batch)
        embed_term = lax.optimization_barrier(jnp.sum(shade_one[None, :, :, None] * back_input, axis=(0, 1, 2)))
        return ((totals[0] + first_term, totals[1] + second_term, totals[2] + embed_term), grad_feature)
    start = (jnp.zeros((3, 3, C, C), jnp.float32), jnp.zeros((3, 3, C, C), jnp.float32), jnp.zeros((C,), jnp.float32))
    totals, grads = lax.scan(per_image, start, (features, shading, cotangent))
    return (grads, totals[0] * scaling, totals[1] * scaling, totals[2] * scaling)
```

```python
import functools
import math

import jax
import jax.numpy as jnp
from jax import lax
from jax.experimental import pallas as pl
from jax.experimental.pallas import tpu as pltpu
from jax.sharding import PartitionSpec as P

MESH = pl.DeviceIdType.MESH
F32 = jnp.float32
BF16 = jnp.bfloat16


def each(count, step):
    if count <= 4:
        for k in range(1, count):
            step(k)
    else:

        def one(k, carry):
            step(k)
            return carry

        lax.fori_loop(1, count, one, 0)


class Exchange:
    def __init__(self, count, make):
        self.count, self.make = count, make

    def start(self):
        each(self.count, lambda k: self.make(k, True).start())

    def wait_recv(self):
        each(self.count, lambda k: self.make(k, False).wait_recv())

    def wait_send(self):
        each(self.count, lambda k: self.make(k, True).wait_send())


class Reduction:
    def __init__(self, place, scale, bufs, sems):
        self.dp, self.space, self.dp_count, self.outer_count = place
        self.core, self.outer = lax.rem(self.space, 2), lax.div(self.space, 2)
        self.full, self.half, self.r1, self.h32, self.h16, self.r2, self.q32, self.q16, self.r3, self.out = bufs
        self.scale = scale
        rows = self.full.shape[1]
        self.quarter = rows // self.dp_count
        self.split = self.quarter % (16 * self.outer_count) == 0
        self.part = self.quarter // self.outer_count if self.split else self.quarter
        pair_s, pair_r, dp_s, dp_r, out_s, out_r, gout_s, gout_r, gdp_s, gdp_r, gpair_s, gpair_r = sems
        core, dp, outer, quarter = self.core, self.dp, self.outer, self.quarter
        sibling = (dp, outer * 2 + 1 - core)

        def rows_of(index, size):
            return pl.ds(pl.multiple_of(index * size, 16), size)

        self.rows_of = rows_of
        make = pltpu.make_async_remote_copy

        def dp_at(k, to):
            return lax.rem(dp + (k if to else self.dp_count - k), self.dp_count)

        def outer_at(k, to):
            return lax.rem(outer + (k if to else self.outer_count - k), self.outer_count)

        def dp_id(k):
            return (dp_at(k, True), self.space)

        def outer_id(k):
            return (dp, outer_at(k, True) * 2 + core)

        def spot(o):
            start = dp * quarter + (o * self.part if self.split else 0)
            return pl.ds(pl.multiple_of(start, 16), self.part)

        self.spot = spot
        self.dp_at = dp_at
        self.s1 = Exchange(2, lambda k, to: make(self.half.at[1 - core], self.r1, pair_s.at[0], pair_r.at[0], device_id=sibling, device_id_type=MESH))
        self.s2_make = lambda k, to: make(
            self.h16.at[rows_of(dp_at(k, True), quarter)], self.r2.at[k - 1], dp_s.at[k - 1], dp_r.at[k - 1], device_id=dp_id(k), device_id_type=MESH
        )
        self.s2 = Exchange(self.dp_count, self.s2_make)
        if self.split:
            self.s3 = Exchange(
                self.outer_count,
                lambda k, to: make(
                    self.q16.at[rows_of(outer_at(k, True), self.part)], self.r3.at[k - 1], out_s.at[k - 1], out_r.at[k - 1], device_id=outer_id(k), device_id_type=MESH
                ),
            )
            self.g3 = Exchange(
                self.outer_count,
                lambda k, to: make(
                    self.out.at[core, spot(outer)],
                    self.out.at[core, spot(outer if to else outer_at(k, False))],
                    gout_s.at[k - 1], gout_r.at[k - 1], device_id=outer_id(k), device_id_type=MESH,
                ),
            )
        else:
            self.s3 = Exchange(
                self.outer_count,
                lambda k, to: make(
                    self.q16, self.r3.at[outer if to else outer_at(k, False)], out_s.at[k - 1], out_r.at[k - 1], device_id=outer_id(k), device_id_type=MESH
                ),
            )
            self.g3 = None
        self.g2 = Exchange(
            self.dp_count,
            lambda k, to: make(
                self.out.at[core, rows_of(dp, quarter)],
                self.out.at[core, rows_of(dp if to else dp_at(k, False), quarter)],
                gdp_s.at[k - 1], gdp_r.at[k - 1], device_id=dp_id(k), device_id_type=MESH,
            ),
        )
        self.g1 = Exchange(
            2,
            lambda k, to: make(
                self.out.at[core], self.out.at[core if to else 1 - core], gpair_s.at[0], gpair_r.at[0], device_id=sibling, device_id_type=MESH
            ),
        )

    def start(self):
        self.s1.start()

    def pair_to_dp(self):
        self.s1.wait_recv()

        def total(index):
            where = self.rows_of(index, self.quarter)
            value = self.full[self.core, where, :] + self.r1[where, :].astype(F32)
            return where, value

        for k in range(1, self.dp_count):
            where, value = total(self.dp_at(k, True))
            self.h16[where, :] = value.astype(BF16)
            self.s2_make(k, True).start()
        _, value = total(self.dp)
        self.h32[...] = value

    def dp_to_outer(self):
        self.s2.wait_recv()
        value = self.h32[...]
        for k in range(1, self.dp_count):
            value = value + self.r2[k - 1].astype(F32)
        self.q32[...] = value
        self.q16[...] = value.astype(BF16)
        self.s3.start()

    def outer_to_gather(self):
        self.s3.wait_recv()
        if self.split:
            value = self.q32[self.rows_of(self.outer, self.part), :]
            for k in range(1, self.outer_count):
                value = value + self.r3[k - 1].astype(F32)
            self.out[self.core, self.spot(self.outer), :] = (value * self.scale).astype(BF16)
            self.g3.start()
        else:
            self.r3[self.outer] = self.q16[...]
            value = lax.fori_loop(0, self.outer_count, lambda j, v: v + self.r3[j].astype(F32), jnp.zeros(self.q32.shape, F32))
            self.out[self.core, self.spot(self.outer), :] = (value * self.scale).astype(BF16)

    def gather_dp(self):
        if self.g3 is not None:
            self.g3.wait_recv()
        self.g2.start()

    def gather_pair(self):
        self.g2.wait_recv()
        self.g1.start()

    def finish(self):
        self.g1.wait_recv()
        for phase in (self.s1, self.s2, self.s3, self.g3, self.g2, self.g1):
            if phase is not None:
                phase.wait_send()


def put(cat, at, value, edge):
    count, width = value.shape
    rows = pl.ds(at, count)
    cat[rows, width : 2 * width] = value.astype(BF16)
    cat[rows, 0:width] = jnp.where(edge == 0, 0.0, pltpu.roll(value, 1, 0)).astype(BF16)
    cat[rows, 2 * width :] = jnp.where(edge == count - 1, 0.0, pltpu.roll(value, count - 1, 0)).astype(BF16)


def kernel(counts, scale, decline, feat, high, cot, w1, w2, embed, gfeat, out1, out2, eout, *scratch):
    dp_count, space_count = counts
    (
        stat, stats, halo_f, halo_c, halo_h, edge_h, shade, wide_shade, xcat, ccat, hcat, xt, at, slope,
        full1, half1, r11, h321, h161, r21, q321, q161, r31,
        full2, half2, r12, h322, h162, r22, q322, q162, r32,
        esum, edp, esp,
        halo_s, halo_r, stat_s, stat_r, edp_s, edp_r, esp_s, esp_r,
    ) = scratch[:43]
    sems1, sems2 = scratch[43:55], scratch[55:67]
    dp, space = lax.axis_index("dp"), lax.axis_index("space")
    strip, cols = high.shape
    width = feat.shape[1]
    pixels = strip * cols
    last = space_count - 1
    make = pltpu.make_async_remote_copy

    barrier = pltpu.get_barrier_semaphore()
    each(dp_count, lambda k: pl.semaphore_signal(barrier, inc=1, device_id=(lax.rem(dp + k, dp_count), space), device_id_type=MESH))
    each(space_count, lambda k: pl.semaphore_signal(barrier, inc=1, device_id=(dp, lax.rem(space + k, space_count)), device_id_type=MESH))

    row_at = lax.broadcasted_iota(jnp.int32, (strip, cols), 0)
    lifted = high[...] + decline * (space * strip + row_at).astype(F32)
    peak = jnp.max(lifted, axis=0, keepdims=True)
    stat[...] = jnp.zeros_like(stat)
    stat[0:1, :] = peak
    stat[1:2, :] = jnp.max(lifted[: strip - 1], axis=0, keepdims=True)
    stat[2:3, :] = lifted[strip - 1 :]
    stat[3:4, :] = lifted[:1]
    pl.semaphore_wait(barrier, dp_count + space_count - 2)

    up = (dp, lax.rem(space + last, space_count))
    down = (dp, lax.rem(space + 1, space_count))
    peaks = Exchange(
        space_count,
        lambda k, to: make(stat, stats.at[k - 1], stat_s.at[k - 1], stat_r.at[k - 1], device_id=(dp, lax.rem(space + k, space_count)), device_id_type=MESH),
    )
    peaks.start()
    tail = pl.ds(pixels - cols, cols)
    sides = []
    for at_sem, (source, halo) in enumerate(((feat, halo_f), (cot, halo_c))):
        sides.append(make(source.at[tail], halo.at[0], halo_s.at[2 * at_sem], halo_r.at[2 * at_sem], device_id=down, device_id_type=MESH))
        sides.append(make(source.at[pl.ds(0, cols)], halo.at[1], halo_s.at[2 * at_sem + 1], halo_r.at[2 * at_sem + 1], device_id=up, device_id_type=MESH))
    for copy in sides:
        copy.start()

    edge = lax.broadcasted_iota(jnp.int32, (cols, width), 0)

    def cot_row(r, carry):
        value = cot[pl.ds(pl.multiple_of(r * cols, cols), cols), :].astype(F32)
        put(ccat, pl.multiple_of((r + 1) * cols, cols), value, edge)
        return carry

    lax.fori_loop(0, strip, cot_row, 0)
    for offset in range(3):
        place = pl.ds(offset * width, width)
        for gap in (((2 - offset) + strip) % (strip + 2), ((2 - offset) + strip + 1) % (strip + 2)):
            at[place, pl.ds(gap * cols, cols)] = jnp.zeros((width, cols), BF16)

    peaks.wait_recv()
    zero = jnp.zeros((1, cols), F32)

    def carry_peak(k, carried):
        return jnp.maximum(carried, jnp.where(k <= space, stats[k - 1, 0:1, :], zero))

    above = lax.fori_loop(2, space_count, carry_peak, zero)
    carried = carry_peak(1, above)
    shade[...] = jnp.zeros_like(shade)
    shade[0:1, :] = jnp.maximum(jnp.maximum(above, stats[0, 1:2, :]) - stats[0, 2:3, :], 0.0)
    running = carried
    for r in range(strip):
        shade[r + 1 : r + 2, :] = jnp.maximum(running - lifted[r : r + 1], 0.0)
        running = jnp.maximum(running, lifted[r : r + 1])
    shade[strip + 1 : strip + 2, :] = jnp.maximum(running - stats[last - 1, 3:4, :], 0.0)
    turned = shade[...].T
    direction = embed[...].astype(F32)

    for copy in sides:
        copy.wait_recv()
    inside = (space > 0, space < last)
    for side, p in ((0, 0), (1, strip + 1)):
        put(ccat, p * cols, jnp.where(inside[side], halo_c[side].astype(F32), 0.0), edge)

    for p in range(strip + 2):
        column = jnp.broadcast_to(turned[:, p : p + 1], (cols, 128))
        if 1 <= p <= strip:
            wide_shade[pl.ds((p - 1) * cols, cols), :] = column
            value = feat[pl.ds((p - 1) * cols, cols), :].astype(F32)
        else:
            value = halo_f[0 if p == 0 else 1].astype(F32)
        value = value + jnp.concatenate([column] * (width // 128), axis=1) * direction
        if p in (0, strip + 1):
            value = jnp.where(inside[0 if p == 0 else 1], value, 0.0)
        put(xcat, p * cols, value, edge)
        flipped = value.astype(BF16).T
        for offset in range(3):
            if 0 <= p - offset < strip:
                xt[pl.ds(offset * width, width), pl.ds((p - offset) * cols, cols)] = flipped

    block = 4
    size = block * cols

    def blocks(step):
        def one(i, carry):
            step(i)
            return carry

        lax.fori_loop(0, strip // block, one, 0)

    def rows(i, shift=0):
        return pl.ds(pl.multiple_of(i * size + shift * cols, cols), size)

    def forward(i):
        total = jnp.zeros((size, width), F32)
        for a in range(3):
            total += jnp.dot(xcat[rows(i, a), :], w1[pl.ds(a * 3 * width, 3 * width), :], preferred_element_type=F32)
        sigma = jax.nn.sigmoid(total)
        slope[rows(i), :] = sigma * (1.0 + total * (1.0 - sigma))
        flipped = (total * sigma).astype(BF16).T
        for a in range(3):
            at[pl.ds(a * width, width), pl.ds(pl.multiple_of(i * size + (2 - a) * cols, cols), size)] = flipped

    def backward(i, cat, weight):
        total = jnp.zeros((size, width), F32)
        for a in range(3):
            for b in range(3):
                total += lax.dot_general(
                    cat[rows(i, a), b * width : (b + 1) * width],
                    weight[pl.ds(((2 - a) * 3 + 2 - b) * width, width), :],
                    (((1,), (1,)), ((), ())),
                    preferred_element_type=F32,
                )
        return total

    def kernel_grad(left, cat, first, count, full, half):
        def one(b, carry):
            value = jnp.dot(
                left[...], cat[pl.ds(first, count), pl.ds(pl.multiple_of((2 - b) * width, width), width)], preferred_element_type=F32
            )
            for a in range(3):
                for side in range(2):
                    piece = value[a * width : (a + 1) * width, side * (width // 2) : (side + 1) * (width // 2)]
                    where = pl.ds(pl.multiple_of((a * 3 + b) * width, width), width)
                    full[side, where, :] = piece
                    half[side, where, :] = piece.astype(BF16)
            return carry

        lax.fori_loop(0, 3, one, 0)

    place = (dp, space, dp_count, space_count // 2)
    first = Reduction(place, scale, (full1, half1, r11, h321, h161, r21, q321, q161, r31, out1), sems1)
    second = Reduction(place, scale, (full2, half2, r12, h322, h162, r22, q322, q162, r32, out2), sems2)

    blocks(forward)
    kernel_grad(at, ccat, 0, (strip + 2) * cols, full2, half2)
    second.start()

    def hidden(i):
        value = backward(i, ccat, w2) * slope[rows(i), :]
        for j in range(block):
            put(hcat, pl.multiple_of(i * size + (j + 1) * cols, cols), value[j * cols : (j + 1) * cols], edge)

    blocks(hidden)
    edge_h[0] = hcat[pl.ds(strip * cols, cols), width : 2 * width]
    edge_h[1] = hcat[pl.ds(cols, cols), width : 2 * width]
    borders = [
        make(edge_h.at[0], halo_h.at[0], halo_s.at[4], halo_r.at[4], device_id=down, device_id_type=MESH),
        make(edge_h.at[1], halo_h.at[1], halo_s.at[5], halo_r.at[5], device_id=up, device_id_type=MESH),
    ]
    for copy in borders:
        copy.start()
    second.pair_to_dp()
    kernel_grad(xt, hcat, cols, pixels, full1, half1)
    first.start()
    for copy in borders:
        copy.wait_recv()
    for side, p in ((0, 0), (1, strip + 1)):
        put(hcat, p * cols, jnp.where(inside[side], halo_h[side].astype(F32), 0.0), edge)
    first.pair_to_dp()
    esum[...] = jnp.zeros_like(esum)

    def inputs(i):
        value = backward(i, hcat, w1)
        gfeat[rows(i), :] = (cot[rows(i), :].astype(F32) + value).astype(BF16)
        lean = wide_shade[rows(i), :]
        weighted = jnp.concatenate([lean] * (width // 128), axis=1) * value
        esum[...] += jnp.sum(weighted.reshape(size // 8, 8, width), axis=0)

    blocks(inputs)
    edp[dp] = esum[...]
    share_dp = Exchange(
        dp_count,
        lambda k, to: make(
            esum, edp.at[dp if to else lax.rem(dp + dp_count - k, dp_count)], edp_s.at[k - 1], edp_r.at[k - 1],
            device_id=(lax.rem(dp + k, dp_count), space), device_id_type=MESH,
        ),
    )
    share_dp.start()
    second.dp_to_outer()
    share_dp.wait_recv()
    value = edp[0]
    for k in range(1, dp_count):
        value = value + edp[k]
    esp[space] = value
    share_space = Exchange(
        space_count,
        lambda k, to: make(
            esp.at[space], esp.at[space if to else lax.rem(space + space_count - k, space_count)], esp_s.at[k - 1], esp_r.at[k - 1],
            device_id=(dp, lax.rem(space + k, space_count)), device_id_type=MESH,
        ),
    )
    share_space.start()
    second.outer_to_gather()
    first.dp_to_outer()
    second.gather_dp()
    first.outer_to_gather()
    share_space.wait_recv()
    value = lax.fori_loop(1, space_count, lambda k, v: v + esp[k], esp[0])
    eout[...] = jnp.sum(value, axis=0, keepdims=True) * scale
    first.gather_dp()
    second.gather_pair()
    first.gather_pair()
    for copy in sides + borders:
        copy.wait_send()
    peaks.wait_send()
    share_dp.wait_send()
    share_space.wait_send()
    second.finish()
    first.finish()


def body(features, heights, cotangent, weight_first, weight_second, shade_embed):
    images, strip, cols, width = features.shape
    dp_count, space_count = lax.axis_size("dp"), lax.axis_size("space")
    total_rows = strip * space_count
    outer = space_count // 2
    scale = 1.0 / math.sqrt(images * dp_count * total_rows * cols)
    pixels = strip * cols
    halo = (strip + 2) * cols
    taps = 9 * width
    lanes = width // 2
    quarter = taps // dp_count
    split = quarter % (16 * outer) == 0
    vmem = pltpu.VMEM
    dma = pltpu.SemaphoreType.DMA
    r3 = (outer - 1, quarter // outer, lanes) if split else (outer, quarter, lanes)
    reduction = [
        vmem((2, taps, lanes), F32), vmem((2, taps, lanes), BF16), vmem((taps, lanes), BF16),
        vmem((quarter, lanes), F32), vmem((taps, lanes), BF16), vmem((dp_count - 1, quarter, lanes), BF16),
        vmem((quarter, lanes), F32), vmem((quarter, lanes), BF16), vmem(r3, BF16),
    ]
    pairs = [1, dp_count - 1, outer - 1, outer - 1, dp_count - 1, 1]
    phase_sems = [dma((count,)) for count in pairs for _ in range(2)]
    scratch = [
        vmem((8, cols), F32), vmem((space_count - 1, 8, cols), F32),
        vmem((2, cols, width), BF16), vmem((2, cols, width), BF16), vmem((2, cols, width), BF16), vmem((2, cols, width), BF16),
        vmem((128, cols), F32), vmem((pixels, 128), F32),
        vmem((halo, 3 * width), BF16), vmem((halo, 3 * width), BF16), vmem((halo, 3 * width), BF16),
        vmem((3 * width, pixels), BF16), vmem((3 * width, halo), BF16), vmem((pixels, width), F32),
        *reduction, *reduction,
        vmem((8, width), F32), vmem((dp_count, 8, width), F32), vmem((space_count, 8, width), F32),
        dma((6,)), dma((6,)), dma((space_count - 1,)), dma((space_count - 1,)),
        dma((dp_count - 1,)), dma((dp_count - 1,)), dma((space_count - 1,)), dma((space_count - 1,)),
        *phase_sems, *phase_sems,
    ]
    spec = pl.BlockSpec(memory_space=pltpu.VMEM)
    gfeat, first, second, total = pl.pallas_call(
        functools.partial(kernel, (dp_count, space_count), scale, 2.0 / total_rows),
        out_shape=(
            jax.ShapeDtypeStruct((pixels, width), BF16),
            jax.ShapeDtypeStruct((2, taps, lanes), BF16),
            jax.ShapeDtypeStruct((2, taps, lanes), BF16),
            jax.ShapeDtypeStruct((1, width), F32),
        ),
        in_specs=[spec] * 6,
        out_specs=(spec,) * 4,
        scratch_shapes=scratch,
        compiler_params=pltpu.CompilerParams(collective_id=0, has_side_effects=True, vmem_limit_bytes=60 * 2**20),
        cost_estimate=pl.CostEstimate(flops=90 * pixels * width * width, bytes_accessed=2**24, transcendentals=pixels * width),
    )(
        features.reshape(pixels, width),
        heights.reshape(strip, cols),
        cotangent.reshape(pixels, width),
        weight_first.reshape(taps, width),
        weight_second.reshape(taps, width),
        shade_embed.reshape(1, width),
    )

    def joined(halves):
        return jnp.concatenate([halves[0], halves[1]], axis=1).astype(F32).reshape(3, 3, width, width)

    return gfeat.reshape(features.shape), joined(first), joined(second), total.reshape(width)


def solution(mesh):
    in_specs = (
        P("dp", "space", None, None),
        P("dp", "space", None),
        P("dp", "space", None, None),
        P(),
        P(),
        P(),
    )
    out_specs = (P("dp", "space", None, None), P(), P(), P())
    return jax.shard_map(body, mesh=mesh, in_specs=in_specs, out_specs=out_specs, check_vma=False)
```

```python
import functools
import math

import jax
import jax.numpy as jnp
from jax import lax
from jax.experimental import pallas as pl
from jax.experimental.pallas import tpu as pltpu
from jax.sharding import PartitionSpec as P

MESH = pl.DeviceIdType.MESH
F32 = jnp.float32
BF16 = jnp.bfloat16
PIECES = 3
DELAYS = (1, 3, 6, 8, 11)


def each(count, step):
    if count <= 4:
        for k in range(1, count):
            step(k)
    else:

        def one(k, carry):
            step(k)
            return carry

        lax.fori_loop(1, count, one, 0)


class Exchange:
    def __init__(self, count, make):
        self.count, self.make = count, make

    def start(self):
        each(self.count, lambda k: self.make(k, True).start())

    def wait_recv(self):
        each(self.count, lambda k: self.make(k, False).wait_recv())

    def wait_send(self):
        each(self.count, lambda k: self.make(k, True).wait_send())


class Reduction:
    def __init__(self, place, scale, base, bufs, sems):
        self.dp, self.space, self.dp_count, self.outer_count = place
        self.core, self.outer = lax.rem(self.space, 2), lax.div(self.space, 2)
        self.full, self.half, self.r1, self.h32, self.h16, self.r2, self.q32, self.q16, self.r3, self.out = bufs
        self.base = base
        self.scale = scale
        rows, lanes = self.full.shape[1:]
        mine = pl.ds(pl.multiple_of(self.core * lanes, lanes), lanes)
        theirs = pl.ds(pl.multiple_of((1 - self.core) * lanes, lanes), lanes)
        self.mine = mine
        self.quarter = rows // self.dp_count
        self.split = self.quarter % (16 * self.outer_count) == 0
        self.part = self.quarter // self.outer_count if self.split else self.quarter
        pair_s, pair_r, dp_s, dp_r, out_s, out_r, gout_s, gout_r, gdp_s, gdp_r, gpair_s, gpair_r = sems
        core, dp, outer, quarter = self.core, self.dp, self.outer, self.quarter
        sibling = (dp, outer * 2 + 1 - core)

        def rows_of(index, size, start=0):
            return pl.ds(pl.multiple_of(start + index * size, 16), size)

        self.rows_of = rows_of
        make = pltpu.make_async_remote_copy

        def dp_at(k, to):
            return lax.rem(dp + (k if to else self.dp_count - k), self.dp_count)

        def outer_at(k, to):
            return lax.rem(outer + (k if to else self.outer_count - k), self.outer_count)

        def dp_id(k):
            return (dp_at(k, True), self.space)

        def outer_id(k):
            return (dp, outer_at(k, True) * 2 + core)

        def spot(o):
            start = base + dp * quarter + (o * self.part if self.split else 0)
            return pl.ds(pl.multiple_of(start, 16), self.part)

        self.spot = spot
        self.dp_at = dp_at
        self.s1 = Exchange(2, lambda k, to: make(self.half.at[1 - core], self.r1, pair_s.at[0], pair_r.at[0], device_id=sibling, device_id_type=MESH))
        self.s2_make = lambda k, to: make(
            self.h16.at[rows_of(dp_at(k, True), quarter)], self.r2.at[k - 1], dp_s.at[k - 1], dp_r.at[k - 1], device_id=dp_id(k), device_id_type=MESH
        )
        self.s2 = Exchange(self.dp_count, self.s2_make)
        if self.split:
            self.s3 = Exchange(
                self.outer_count,
                lambda k, to: make(
                    self.q16.at[rows_of(outer_at(k, True), self.part)], self.r3.at[k - 1], out_s.at[k - 1], out_r.at[k - 1], device_id=outer_id(k), device_id_type=MESH
                ),
            )
            self.g3 = Exchange(
                self.outer_count,
                lambda k, to: make(
                    self.out.at[spot(outer), mine],
                    self.out.at[spot(outer if to else outer_at(k, False)), mine],
                    gout_s.at[k - 1], gout_r.at[k - 1], device_id=outer_id(k), device_id_type=MESH,
                ),
            )
        else:
            self.s3 = Exchange(
                self.outer_count,
                lambda k, to: make(
                    self.q16, self.r3.at[outer if to else outer_at(k, False)], out_s.at[k - 1], out_r.at[k - 1], device_id=outer_id(k), device_id_type=MESH
                ),
            )
            self.g3 = None
        self.g2 = Exchange(
            self.dp_count,
            lambda k, to: make(
                self.out.at[rows_of(dp, quarter, base), mine],
                self.out.at[rows_of(dp if to else dp_at(k, False), quarter, base), mine],
                gdp_s.at[k - 1], gdp_r.at[k - 1], device_id=dp_id(k), device_id_type=MESH,
            ),
        )
        self.g1 = Exchange(
            2,
            lambda k, to: make(
                self.out.at[pl.ds(base, rows), mine], self.out.at[pl.ds(base, rows), mine if to else theirs], gpair_s.at[0], gpair_r.at[0], device_id=sibling, device_id_type=MESH
            ),
        )

    def start(self):
        self.s1.start()

    def pair_to_dp(self):
        self.s1.wait_recv()

        def total(index):
            where = self.rows_of(index, self.quarter)
            value = self.full[self.core, where, :] + self.r1[where, :].astype(F32)
            return where, value

        for k in range(1, self.dp_count):
            where, value = total(self.dp_at(k, True))
            self.h16[where, :] = value.astype(BF16)
            self.s2_make(k, True).start()
        _, value = total(self.dp)
        self.h32[...] = value

    def dp_to_outer(self):
        self.s2.wait_recv()
        value = self.h32[...]
        for k in range(1, self.dp_count):
            value = value + self.r2[k - 1].astype(F32)
        self.q32[...] = value
        self.q16[...] = value.astype(BF16)
        self.s3.start()

    def outer_to_gather(self):
        self.s3.wait_recv()
        if self.split:
            value = self.q32[self.rows_of(self.outer, self.part), :]
            for k in range(1, self.outer_count):
                value = value + self.r3[k - 1].astype(F32)
            self.out[self.spot(self.outer), self.mine] = (value * self.scale).astype(BF16)
            self.g3.start()
        else:
            self.r3[self.outer] = self.q16[...]
            value = lax.fori_loop(0, self.outer_count, lambda j, v: v + self.r3[j].astype(F32), jnp.zeros(self.q32.shape, F32))
            self.out[self.spot(self.outer), self.mine] = (value * self.scale).astype(BF16)

    def gather_dp(self):
        if self.g3 is not None:
            self.g3.wait_recv()
        self.g2.start()

    def gather_pair(self):
        self.g2.wait_recv()
        self.g1.start()

    def finish(self):
        self.g1.wait_recv()
        for phase in (self.s1, self.s2, self.s3, self.g3, self.g2, self.g1):
            if phase is not None:
                phase.wait_send()


def put(cat, at, value, edge):
    count, width = value.shape
    rows = pl.ds(at, count)
    cat[rows, width : 2 * width] = value.astype(BF16)
    cat[rows, 0:width] = jnp.where(edge == 0, 0.0, pltpu.roll(value, 1, 0)).astype(BF16)
    cat[rows, 2 * width :] = jnp.where(edge == count - 1, 0.0, pltpu.roll(value, count - 1, 0)).astype(BF16)


def kernel(counts, scale, decline, feat, high, cot, w1, w2, embed, gfeat, out1, out2, eout, *scratch):
    dp_count, space_count = counts
    (
        stat, stats, halo_f, halo_c, halo_h, edge_h, shade, wide_shade, xcat, ccat, hcat, xt, at, back,
        esum, edp, esp,
        halo_s, halo_r, stat_s, stat_r, edp_s, edp_r, esp_s, esp_r,
    ) = scratch[:25]
    groups, sems = scratch[25 : 25 + 18 * PIECES], scratch[25 + 18 * PIECES :]
    dp, space = lax.axis_index("dp"), lax.axis_index("space")
    strip, cols = high.shape
    width = feat.shape[1]
    pixels = strip * cols
    last = space_count - 1
    make = pltpu.make_async_remote_copy

    barrier = pltpu.get_barrier_semaphore()
    each(dp_count, lambda k: pl.semaphore_signal(barrier, inc=1, device_id=(lax.rem(dp + k, dp_count), space), device_id_type=MESH))
    each(space_count, lambda k: pl.semaphore_signal(barrier, inc=1, device_id=(dp, lax.rem(space + k, space_count)), device_id_type=MESH))

    row_at = lax.broadcasted_iota(jnp.int32, (strip, cols), 0)
    lifted = high[...] + decline * (space * strip + row_at).astype(F32)
    peak = jnp.max(lifted, axis=0, keepdims=True)
    stat[...] = jnp.zeros_like(stat)
    stat[0:1, :] = peak
    stat[1:2, :] = jnp.max(lifted[: strip - 1], axis=0, keepdims=True)
    stat[2:3, :] = lifted[strip - 1 :]
    stat[3:4, :] = lifted[:1]
    pl.semaphore_wait(barrier, dp_count + space_count - 2)

    up = (dp, lax.rem(space + last, space_count))
    down = (dp, lax.rem(space + 1, space_count))
    peaks = Exchange(
        space_count,
        lambda k, to: make(stat, stats.at[k - 1], stat_s.at[k - 1], stat_r.at[k - 1], device_id=(dp, lax.rem(space + k, space_count)), device_id_type=MESH),
    )
    peaks.start()
    inside = (space > 0, space < last)

    def sides_of(bottom, top, halo, at_sem):
        return [
            (space < last, space > 0, make(bottom, halo.at[0], halo_s.at[at_sem], halo_r.at[at_sem], device_id=down, device_id_type=MESH)),
            (space > 0, space < last, make(top, halo.at[1], halo_s.at[at_sem + 1], halo_r.at[at_sem + 1], device_id=up, device_id_type=MESH)),
        ]

    def start_sides(copies):
        for sends, _, copy in copies:
            pl.when(sends)(copy.start)

    def wait_sides(copies):
        for _, gets, copy in copies:
            pl.when(gets)(copy.wait_recv)

    def end_sides(copies):
        for sends, _, copy in copies:
            pl.when(sends)(copy.wait_send)

    tail, front = pl.ds(pixels - cols, cols), pl.ds(0, cols)
    sides = sides_of(feat.at[tail], feat.at[front], halo_f, 0) + sides_of(cot.at[tail], cot.at[front], halo_c, 2)
    for edge_halo in (halo_f, halo_c, halo_h):
        for side in range(2):

            @pl.when(jnp.logical_not(inside[side]))
            def _():
                edge_halo[side] = jnp.zeros((cols, width), BF16)

    start_sides(sides)

    edge = lax.broadcasted_iota(jnp.int32, (cols, width), 0)

    def cot_row(r, carry):
        value = cot[pl.ds(pl.multiple_of(r * cols, cols), cols), :].astype(F32)
        put(ccat, pl.multiple_of((r + 1) * cols, cols), value, edge)
        return carry

    lax.fori_loop(0, strip, cot_row, 0)
    for offset in range(3):
        place = pl.ds(offset * width, width)
        for gap in (((2 - offset) + strip) % (strip + 2), ((2 - offset) + strip + 1) % (strip + 2)):
            at[place, pl.ds(gap * cols, cols)] = jnp.zeros((width, cols), BF16)

    block = 4
    size = block * cols

    def rows(i, shift=0):
        return pl.ds(pl.multiple_of(i * size + shift * cols, cols), size)

    def backward(i, cat, weight):
        total = jnp.zeros((size, width), F32)
        for a in range(3):
            for b in range(3):
                total += lax.dot_general(
                    cat[rows(i, a), b * width : (b + 1) * width],
                    weight[pl.ds(((2 - a) * 3 + 2 - b) * width, width), :],
                    (((1,), (1,)), ((), ())),
                    preferred_element_type=F32,
                )
        return total

    def loop(start, stop, step):
        def one(i, carry):
            step(i)
            return carry

        lax.fori_loop(start, stop, one, 0)

    def back_act(i):
        back[rows(i), :] = backward(i, ccat, w2)

    loop(1, strip // block - 1, back_act)

    peaks.wait_recv()
    zero = jnp.zeros((1, cols), F32)

    def carry_peak(k, carried):
        return jnp.maximum(carried, jnp.where(k <= space, stats[k - 1, 0:1, :], zero))

    above = lax.fori_loop(2, space_count, carry_peak, zero)
    carried = carry_peak(1, above)
    shade[...] = jnp.zeros_like(shade)
    shade[0:1, :] = jnp.maximum(jnp.maximum(above, stats[0, 1:2, :]) - stats[0, 2:3, :], 0.0)
    running = carried
    for r in range(strip):
        shade[r + 1 : r + 2, :] = jnp.maximum(running - lifted[r : r + 1], 0.0)
        running = jnp.maximum(running, lifted[r : r + 1])
    shade[strip + 1 : strip + 2, :] = jnp.maximum(running - stats[last - 1, 3:4, :], 0.0)
    turned = shade[...].T
    direction = embed[...].astype(F32).reshape(1, width)

    wait_sides(sides)
    for side, p in ((0, 0), (1, strip + 1)):
        put(ccat, p * cols, jnp.where(inside[side], halo_c[side].astype(F32), 0.0), edge)

    back_act(0)
    back_act(strip // block - 1)

    for p in range(strip + 2):
        column = jnp.broadcast_to(turned[:, p : p + 1], (cols, 128))
        if 1 <= p <= strip:
            wide_shade[pl.ds((p - 1) * cols, cols), :] = column
            value = feat[pl.ds((p - 1) * cols, cols), :].astype(F32)
        else:
            value = halo_f[0 if p == 0 else 1].astype(F32)
        value = value + jnp.concatenate([column] * (width // 128), axis=1) * direction
        if p in (0, strip + 1):
            value = jnp.where(inside[0 if p == 0 else 1], value, 0.0)
        put(xcat, p * cols, value, edge)
        flipped = value.astype(BF16).T
        for offset in range(3):
            if 0 <= p - offset < strip:
                xt[pl.ds(offset * width, width), pl.ds((p - offset) * cols, cols)] = flipped

    def kernel_grad(left, cat, first, count, b, full, half, row):
        value = jnp.dot(left[...], cat[pl.ds(first, count), (2 - b) * width : (3 - b) * width], preferred_element_type=F32)
        for side in range(2):
            piece = value[:, side * (width // 2) : (side + 1) * (width // 2)]
            full[side, pl.ds(row, 3 * width), :] = piece
            half[side, pl.ds(row, 3 * width), :] = piece.astype(BF16)

    def forward(i):
        total = jnp.zeros((size, width), F32)
        for a in range(3):
            total += jnp.dot(xcat[rows(i, a), :], w1[pl.ds(a * 3 * width, 3 * width), :], preferred_element_type=F32)
        sigma = jax.nn.sigmoid(total)
        flipped = (total * sigma).astype(BF16).T
        for a in range(3):
            at[pl.ds(a * width, width), pl.ds(pl.multiple_of(i * size + (2 - a) * cols, cols), size)] = flipped
        value = back[rows(i), :] * (sigma * (1.0 + total * (1.0 - sigma)))
        for j in range(block):
            put(hcat, pl.multiple_of(i * size + (j + 1) * cols, cols), value[j * cols : (j + 1) * cols], edge)

    def inputs(i):
        value = backward(i, hcat, w1)
        gfeat[rows(i), :] = (cot[rows(i), :].astype(F32) + value).astype(BF16)
        lean = wide_shade[rows(i), :]
        weighted = jnp.concatenate([lean] * (width // 128), axis=1) * value
        esum[...] += jnp.sum(weighted.reshape(size // 8, 8, width), axis=0)

    loop(0, strip // block, forward)
    edge_h[0] = hcat[pl.ds(strip * cols, cols), width : 2 * width]
    edge_h[1] = hcat[pl.ds(cols, cols), width : 2 * width]
    borders = sides_of(edge_h.at[0], edge_h.at[1], halo_h, 4)
    start_sides(borders)

    place = (dp, space, dp_count, space_count // 2)
    depth = 3 // PIECES
    pieces = []
    for index in range(2 * PIECES):
        of, b0 = divmod(index, PIECES)
        base = b0 * depth * 3 * width
        bufs = groups[index * 9 : index * 9 + 9]
        pieces.append(Reduction(place, scale, base, (*bufs, (out2, out1)[of]), sems[index * 12 : index * 12 + 12]))

    def grad_piece(index):
        of, b0 = divmod(index, PIECES)
        red = pieces[index]
        for step in range(depth):
            b = b0 * depth + step
            left, cat, first, count = ((at, ccat, 0, (strip + 2) * cols), (xt, hcat, cols, pixels))[of]
            kernel_grad(left, cat, first, count, b, red.full, red.half, step * 3 * width)
        red.start()

    share_dp = Exchange(
        dp_count,
        lambda k, to: make(
            esum, edp.at[dp if to else lax.rem(dp + dp_count - k, dp_count)], edp_s.at[k - 1], edp_r.at[k - 1],
            device_id=(lax.rem(dp + k, dp_count), space), device_id_type=MESH,
        ),
    )
    share_space = Exchange(
        space_count,
        lambda k, to: make(
            esp.at[space], esp.at[space if to else lax.rem(space + space_count - k, space_count)], esp_s.at[k - 1], esp_r.at[k - 1],
            device_id=(dp, lax.rem(space + k, space_count)), device_id_type=MESH,
        ),
    )

    def borders_in():
        wait_sides(borders)
        for side, p in ((0, 0), (1, strip + 1)):
            put(hcat, p * cols, jnp.where(inside[side], halo_h[side].astype(F32), 0.0), edge)
        esum[...] = jnp.zeros_like(esum)

    def embed_dp():
        edp[dp] = esum[...]
        share_dp.start()

    def embed_space():
        share_dp.wait_recv()
        value = edp[0]
        for k in range(1, dp_count):
            value = value + edp[k]
        esp[space] = value
        share_space.start()

    def embed_end():
        share_space.wait_recv()
        value = lax.fori_loop(1, space_count, lambda k, v: v + esp[k], esp[0])
        eout[...] = jnp.sum(value, axis=0, keepdims=True) * scale

    events = []
    tick = 3 // PIECES
    for index, red in enumerate(pieces):
        at_tick = index * tick
        events.append((at_tick, 1, functools.partial(grad_piece, index)))
        ready = at_tick + tick
        for delay, step in zip(DELAYS, (red.pair_to_dp, red.dp_to_outer, red.outer_to_gather, red.gather_dp, red.gather_pair)):
            events.append((ready + delay, 0, step))
    events.append((6, 2, borders_in))
    for i in range(strip // block):
        events.append((6 + i, 3, functools.partial(inputs, i)))
    finished = 6 + strip // block
    events += [(finished, 0, embed_dp), (finished + 4, 0, embed_space), (finished + 9, 0, embed_end)]
    for _, _, step in sorted(events, key=lambda event: event[:2]):
        step()
    end_sides(sides + borders)
    peaks.wait_send()
    share_dp.wait_send()
    share_space.wait_send()
    for red in pieces:
        red.finish()


def body(features, heights, cotangent, weight_first, weight_second, shade_embed):
    images, strip, cols, width = features.shape
    dp_count, space_count = lax.axis_size("dp"), lax.axis_size("space")
    total_rows = strip * space_count
    outer = space_count // 2
    scale = 1.0 / math.sqrt(images * dp_count * total_rows * cols)
    pixels = strip * cols
    halo = (strip + 2) * cols
    taps = 9 * width
    lanes = width // 2
    piece = taps // PIECES
    quarter = piece // dp_count
    split = quarter % (16 * outer) == 0
    vmem = pltpu.VMEM
    dma = pltpu.SemaphoreType.DMA
    r3 = (outer - 1, quarter // outer, lanes) if split else (outer, quarter, lanes)
    reduction = [
        vmem((2, piece, lanes), F32), vmem((2, piece, lanes), BF16), vmem((piece, lanes), BF16),
        vmem((quarter, lanes), F32), vmem((piece, lanes), BF16), vmem((dp_count - 1, quarter, lanes), BF16),
        vmem((quarter, lanes), F32), vmem((quarter, lanes), BF16), vmem(r3, BF16),
    ]
    pairs = [1, dp_count - 1, outer - 1, outer - 1, dp_count - 1, 1]
    phase_sems = [dma((count,)) for count in pairs for _ in range(2)]
    scratch = [
        vmem((8, cols), F32), vmem((space_count - 1, 8, cols), F32),
        vmem((2, cols, width), BF16), vmem((2, cols, width), BF16), vmem((2, cols, width), BF16), vmem((2, cols, width), BF16),
        vmem((128, cols), F32), vmem((pixels, 128), F32),
        vmem((halo, 3 * width), BF16), vmem((halo, 3 * width), BF16), vmem((halo, 3 * width), BF16),
        vmem((3 * width, pixels), BF16), vmem((3 * width, halo), BF16), vmem((pixels, width), F32),
        vmem((8, width), F32), vmem((dp_count, 8, width), F32), vmem((space_count, 8, width), F32),
        dma((6,)), dma((6,)), dma((space_count - 1,)), dma((space_count - 1,)),
        dma((dp_count - 1,)), dma((dp_count - 1,)), dma((space_count - 1,)), dma((space_count - 1,)),
        *(reduction * (2 * PIECES)),
        *(phase_sems * (2 * PIECES)),
    ]
    spec = pl.BlockSpec(memory_space=pltpu.VMEM)
    gfeat, first, second, total = pl.pallas_call(
        functools.partial(kernel, (dp_count, space_count), scale, 2.0 / total_rows),
        out_shape=(
            jax.ShapeDtypeStruct((pixels, width), BF16),
            jax.ShapeDtypeStruct((taps, width), BF16),
            jax.ShapeDtypeStruct((taps, width), BF16),
            jax.ShapeDtypeStruct((1, width), F32),
        ),
        in_specs=[spec] * 6,
        out_specs=(spec,) * 4,
        scratch_shapes=scratch,
        compiler_params=pltpu.CompilerParams(collective_id=0, has_side_effects=True, vmem_limit_bytes=60 * 2**20),
        cost_estimate=pl.CostEstimate(flops=90 * pixels * width * width, bytes_accessed=2**24, transcendentals=pixels * width),
    )(
        features.reshape(pixels, width),
        heights.reshape(strip, cols),
        cotangent.reshape(pixels, width),
        weight_first.reshape(taps, width),
        weight_second.reshape(taps, width),
        shade_embed,
    )

    def joined(pieces):
        return jnp.swapaxes(pieces.reshape(3, 3, width, width), 0, 1).astype(F32)

    return gfeat.reshape(features.shape), joined(first), joined(second), total.reshape(width)


def solution(mesh):
    in_specs = (
        P("dp", "space", None, None),
        P("dp", "space", None),
        P("dp", "space", None, None),
        P(),
        P(),
        P(),
    )
    out_specs = (P("dp", "space", None, None), P(), P(), P())
    return jax.shard_map(body, mesh=mesh, in_specs=in_specs, out_specs=out_specs, check_vma=False)
```

```python
import functools
import math

import jax
import jax.numpy as jnp
from jax import lax
from jax.experimental import pallas as pl
from jax.experimental.pallas import tpu as pltpu
from jax.sharding import PartitionSpec as P

MESH = pl.DeviceIdType.MESH
F32 = jnp.float32
BF16 = jnp.bfloat16
PIECES = 3
DELAYS = (1, 3, 6, 8, 11)


def each(count, step):
    if count <= 4:
        for k in range(1, count):
            step(k)
    else:

        def one(k, carry):
            step(k)
            return carry

        lax.fori_loop(1, count, one, 0)


class Exchange:
    def __init__(self, count, make):
        self.count, self.make = count, make

    def start(self):
        each(self.count, lambda k: self.make(k, True).start())

    def wait_recv(self):
        each(self.count, lambda k: self.make(k, False).wait_recv())

    def wait_send(self):
        each(self.count, lambda k: self.make(k, True).wait_send())


class Reduction:
    def __init__(self, place, scale, base, bufs, sems):
        self.dp, self.space, self.dp_count, self.outer_count = place
        self.core, self.outer = lax.rem(self.space, 2), lax.div(self.space, 2)
        self.full, self.half, self.r1, self.h32, self.h16, self.r2, self.q32, self.q16, self.r3, self.out = bufs
        self.base = base
        self.scale = scale
        rows, lanes = self.full.shape[2:]
        mine = pl.ds(pl.multiple_of(self.core * lanes, lanes), lanes)
        theirs = pl.ds(pl.multiple_of((1 - self.core) * lanes, lanes), lanes)
        self.mine = mine
        self.quarter = rows // self.dp_count
        self.split = self.quarter % (16 * self.outer_count) == 0
        self.part = self.quarter // self.outer_count if self.split else self.quarter
        pair_s, pair_r, dp_s, dp_r, out_s, out_r, gout_s, gout_r, gdp_s, gdp_r, gpair_s, gpair_r = sems
        core, dp, outer, quarter = self.core, self.dp, self.outer, self.quarter
        sibling = (dp, outer * 2 + 1 - core)

        def rows_of(index, size):
            return pl.ds(pl.multiple_of(index * size, 16), size)

        self.rows_of = rows_of
        make = pltpu.make_async_remote_copy

        def dp_at(k, to):
            return lax.rem(dp + (k if to else self.dp_count - k), self.dp_count)

        def outer_at(k, to):
            return lax.rem(outer + (k if to else self.outer_count - k), self.outer_count)

        def dp_id(k):
            return (dp_at(k, True), self.space)

        def outer_id(k):
            return (dp, outer_at(k, True) * 2 + core)

        def spot(o):
            start = dp * quarter + (o * self.part if self.split else 0)
            return pl.ds(pl.multiple_of(start, 16), self.part)

        self.spot = spot
        self.dp_at = dp_at
        self.s1 = Exchange(2, lambda k, to: make(self.half.at[1 - core], self.r1, pair_s.at[0], pair_r.at[0], device_id=sibling, device_id_type=MESH))
        self.s2_make = lambda k, to: make(
            self.h16.at[:, rows_of(dp_at(k, True), quarter)], self.r2.at[k - 1], dp_s.at[k - 1], dp_r.at[k - 1], device_id=dp_id(k), device_id_type=MESH
        )
        self.s2 = Exchange(self.dp_count, self.s2_make)
        if self.split:
            self.s3 = Exchange(
                self.outer_count,
                lambda k, to: make(
                    self.q16.at[:, rows_of(outer_at(k, True), self.part)], self.r3.at[k - 1], out_s.at[k - 1], out_r.at[k - 1], device_id=outer_id(k), device_id_type=MESH
                ),
            )
            self.g3 = Exchange(
                self.outer_count,
                lambda k, to: make(
                    self.out.at[:, base, spot(outer), mine],
                    self.out.at[:, base, spot(outer if to else outer_at(k, False)), mine],
                    gout_s.at[k - 1], gout_r.at[k - 1], device_id=outer_id(k), device_id_type=MESH,
                ),
            )
        else:
            self.s3 = Exchange(
                self.outer_count,
                lambda k, to: make(
                    self.q16, self.r3.at[outer if to else outer_at(k, False)], out_s.at[k - 1], out_r.at[k - 1], device_id=outer_id(k), device_id_type=MESH
                ),
            )
            self.g3 = None
        self.g2 = Exchange(
            self.dp_count,
            lambda k, to: make(
                self.out.at[:, base, rows_of(dp, quarter), mine],
                self.out.at[:, base, rows_of(dp if to else dp_at(k, False), quarter), mine],
                gdp_s.at[k - 1], gdp_r.at[k - 1], device_id=dp_id(k), device_id_type=MESH,
            ),
        )
        self.g1 = Exchange(
            2,
            lambda k, to: make(
                self.out.at[:, base, :, mine], self.out.at[:, base, :, mine if to else theirs], gpair_s.at[0], gpair_r.at[0], device_id=sibling, device_id_type=MESH
            ),
        )

    def start(self):
        self.s1.start()

    def pair_to_dp(self):
        self.s1.wait_recv()

        def total(index):
            where = self.rows_of(index, self.quarter)
            value = self.full[self.core, :, where, :] + self.r1[:, where, :].astype(F32)
            return where, value

        for k in range(1, self.dp_count):
            where, value = total(self.dp_at(k, True))
            self.h16[:, where, :] = value.astype(BF16)
            self.s2_make(k, True).start()
        _, value = total(self.dp)
        self.h32[...] = value

    def dp_to_outer(self):
        self.s2.wait_recv()
        value = self.h32[...]
        for k in range(1, self.dp_count):
            value = value + self.r2[k - 1].astype(F32)
        self.q32[...] = value
        self.q16[...] = value.astype(BF16)
        self.s3.start()

    def outer_to_gather(self):
        self.s3.wait_recv()
        if self.split:
            value = self.q32[:, self.rows_of(self.outer, self.part), :]
            for k in range(1, self.outer_count):
                value = value + self.r3[k - 1].astype(F32)
            self.out[:, self.base, self.spot(self.outer), self.mine] = (value * self.scale).astype(BF16)
            self.g3.start()
        else:
            self.r3[self.outer] = self.q16[...]
            value = lax.fori_loop(0, self.outer_count, lambda j, v: v + self.r3[j].astype(F32), jnp.zeros(self.q32.shape, F32))
            self.out[:, self.base, self.spot(self.outer), self.mine] = (value * self.scale).astype(BF16)

    def gather_dp(self):
        if self.g3 is not None:
            self.g3.wait_recv()
        self.g2.start()

    def gather_pair(self):
        self.g2.wait_recv()
        self.g1.start()

    def finish(self):
        self.g1.wait_recv()
        for phase in (self.s1, self.s2, self.s3, self.g3, self.g2, self.g1):
            if phase is not None:
                phase.wait_send()


def put(cat, at, value, edge):
    count, width = value.shape
    rows = pl.ds(at, count)
    cat[rows, width : 2 * width] = value.astype(BF16)
    cat[rows, 0:width] = jnp.where(edge == 0, 0.0, pltpu.roll(value, 1, 0)).astype(BF16)
    cat[rows, 2 * width :] = jnp.where(edge == count - 1, 0.0, pltpu.roll(value, count - 1, 0)).astype(BF16)


def kernel(counts, scale, decline, feat, high, cot, w1_in, w2_in, embed, gfeat, out1, out2, eout, *scratch):
    dp_count, space_count = counts
    (
        stat, stats, halo_f, halo_c, halo_h, edge_h, shade, wide_shade, xcat, ccat, hcat, xt, at, back,
        esum, edp, esp,
        halo_s, halo_r, stat_s, stat_r, edp_s, edp_r, esp_s, esp_r, w1, w2, w_s,
    ) = scratch[:28]
    groups, sems = scratch[28 : 28 + 18 * PIECES], scratch[28 + 18 * PIECES :]
    load1 = pltpu.make_async_copy(w1_in, w1, w_s.at[0])
    load2 = pltpu.make_async_copy(w2_in, w2, w_s.at[1])
    load2.start()
    load1.start()
    dp, space = lax.axis_index("dp"), lax.axis_index("space")
    strip, cols = high.shape
    width = feat.shape[1]
    pixels = strip * cols
    last = space_count - 1
    make = pltpu.make_async_remote_copy

    barrier = pltpu.get_barrier_semaphore()
    each(dp_count, lambda k: pl.semaphore_signal(barrier, inc=1, device_id=(lax.rem(dp + k, dp_count), space), device_id_type=MESH))
    each(space_count, lambda k: pl.semaphore_signal(barrier, inc=1, device_id=(dp, lax.rem(space + k, space_count)), device_id_type=MESH))

    row_at = lax.broadcasted_iota(jnp.int32, (strip, cols), 0)
    lifted = high[...] + decline * (space * strip + row_at).astype(F32)
    peak = jnp.max(lifted, axis=0, keepdims=True)
    stat[...] = jnp.zeros_like(stat)
    stat[0:1, :] = peak
    stat[1:2, :] = jnp.max(lifted[: strip - 1], axis=0, keepdims=True)
    stat[2:3, :] = lifted[strip - 1 :]
    stat[3:4, :] = lifted[:1]
    pl.semaphore_wait(barrier, dp_count + space_count - 2)

    up = (dp, lax.rem(space + last, space_count))
    down = (dp, lax.rem(space + 1, space_count))
    peaks = Exchange(
        space_count,
        lambda k, to: make(stat, stats.at[k - 1], stat_s.at[k - 1], stat_r.at[k - 1], device_id=(dp, lax.rem(space + k, space_count)), device_id_type=MESH),
    )
    peaks.start()
    inside = (space > 0, space < last)

    def sides_of(bottom, top, halo, at_sem):
        return [
            (space < last, space > 0, make(bottom, halo.at[0], halo_s.at[at_sem], halo_r.at[at_sem], device_id=down, device_id_type=MESH)),
            (space > 0, space < last, make(top, halo.at[1], halo_s.at[at_sem + 1], halo_r.at[at_sem + 1], device_id=up, device_id_type=MESH)),
        ]

    def start_sides(copies):
        for sends, _, copy in copies:
            pl.when(sends)(copy.start)

    def wait_sides(copies):
        for _, gets, copy in copies:
            pl.when(gets)(copy.wait_recv)

    def end_sides(copies):
        for sends, _, copy in copies:
            pl.when(sends)(copy.wait_send)

    tail, front = pl.ds(pixels - cols, cols), pl.ds(0, cols)
    sides = sides_of(feat.at[tail], feat.at[front], halo_f, 0) + sides_of(cot.at[tail], cot.at[front], halo_c, 2)
    for edge_halo in (halo_f, halo_c, halo_h):
        for side in range(2):

            @pl.when(jnp.logical_not(inside[side]))
            def _():
                edge_halo[side] = jnp.zeros((cols, width), BF16)

    start_sides(sides)

    edge = lax.broadcasted_iota(jnp.int32, (cols, width), 0)

    def cot_row(r, carry):
        value = cot[pl.ds(pl.multiple_of(r * cols, cols), cols), :].astype(F32)
        put(ccat, pl.multiple_of((r + 1) * cols, cols), value, edge)
        return carry

    lax.fori_loop(0, strip, cot_row, 0)
    for offset in range(3):
        place = pl.ds(offset * width, width)
        for gap in (((2 - offset) + strip) % (strip + 2), ((2 - offset) + strip + 1) % (strip + 2)):
            at[place, pl.ds(gap * cols, cols)] = jnp.zeros((width, cols), BF16)

    block = 4
    size = block * cols

    def rows(i, shift=0):
        return pl.ds(pl.multiple_of(i * size + shift * cols, cols), size)

    def backward(i, cat, weight):
        total = jnp.zeros((size, width), F32)
        for a in range(3):
            for b in range(3):
                total += lax.dot_general(
                    cat[rows(i, a), b * width : (b + 1) * width],
                    weight[pl.ds(((2 - a) * 3 + 2 - b) * width, width), :],
                    (((1,), (1,)), ((), ())),
                    preferred_element_type=F32,
                )
        return total

    def loop(start, stop, step):
        def one(i, carry):
            step(i)
            return carry

        lax.fori_loop(start, stop, one, 0)

    def back_act(i):
        back[rows(i), :] = backward(i, ccat, w2)

    load2.wait()
    loop(1, strip // block - 1, back_act)

    peaks.wait_recv()
    zero = jnp.zeros((1, cols), F32)

    def carry_peak(k, carried):
        return jnp.maximum(carried, jnp.where(k <= space, stats[k - 1, 0:1, :], zero))

    above = lax.fori_loop(2, space_count, carry_peak, zero)
    carried = carry_peak(1, above)
    shade[...] = jnp.zeros_like(shade)
    shade[0:1, :] = jnp.maximum(jnp.maximum(above, stats[0, 1:2, :]) - stats[0, 2:3, :], 0.0)
    running = carried
    for r in range(strip):
        shade[r + 1 : r + 2, :] = jnp.maximum(running - lifted[r : r + 1], 0.0)
        running = jnp.maximum(running, lifted[r : r + 1])
    shade[strip + 1 : strip + 2, :] = jnp.maximum(running - stats[last - 1, 3:4, :], 0.0)
    turned = shade[...].T
    direction = embed[...].astype(F32).reshape(1, width)

    wait_sides(sides)
    for side, p in ((0, 0), (1, strip + 1)):
        put(ccat, p * cols, jnp.where(inside[side], halo_c[side].astype(F32), 0.0), edge)

    back_act(0)
    back_act(strip // block - 1)

    for p in range(strip + 2):
        column = jnp.broadcast_to(turned[:, p : p + 1], (cols, 128))
        if 1 <= p <= strip:
            wide_shade[pl.ds((p - 1) * cols, cols), :] = column
            value = feat[pl.ds((p - 1) * cols, cols), :].astype(F32)
        else:
            value = halo_f[0 if p == 0 else 1].astype(F32)
        value = value + jnp.concatenate([column] * (width // 128), axis=1) * direction
        if p in (0, strip + 1):
            value = jnp.where(inside[0 if p == 0 else 1], value, 0.0)
        put(xcat, p * cols, value, edge)
        flipped = value.astype(BF16).T
        for offset in range(3):
            if 0 <= p - offset < strip:
                xt[pl.ds(offset * width, width), pl.ds((p - offset) * cols, cols)] = flipped

    def kernel_grad(left, cat, first, count, b, full, half):
        value = jnp.dot(left[...], cat[pl.ds(first, count), (2 - b) * width : (3 - b) * width], preferred_element_type=F32)
        for side in range(2):
            piece = value[:, side * (width // 2) : (side + 1) * (width // 2)].reshape(3, width, width // 2)
            full[side] = piece
            half[side] = piece.astype(BF16)

    def forward(i):
        total = jnp.zeros((size, width), F32)
        for a in range(3):
            total += jnp.dot(xcat[rows(i, a), :], w1[pl.ds(a * 3 * width, 3 * width), :], preferred_element_type=F32)
        sigma = jax.nn.sigmoid(total)
        flipped = (total * sigma).astype(BF16).T
        for a in range(3):
            at[pl.ds(a * width, width), pl.ds(pl.multiple_of(i * size + (2 - a) * cols, cols), size)] = flipped
        value = back[rows(i), :] * (sigma * (1.0 + total * (1.0 - sigma)))
        for j in range(block):
            put(hcat, pl.multiple_of(i * size + (j + 1) * cols, cols), value[j * cols : (j + 1) * cols], edge)

    def inputs(i):
        value = backward(i, hcat, w1)
        gfeat[rows(i), :] = (cot[rows(i), :].astype(F32) + value).astype(BF16)
        lean = wide_shade[rows(i), :]
        weighted = jnp.concatenate([lean] * (width // 128), axis=1) * value
        esum[...] += jnp.sum(weighted.reshape(size // 8, 8, width), axis=0)

    load1.wait()
    loop(0, strip // block, forward)
    edge_h[0] = hcat[pl.ds(strip * cols, cols), width : 2 * width]
    edge_h[1] = hcat[pl.ds(cols, cols), width : 2 * width]
    borders = sides_of(edge_h.at[0], edge_h.at[1], halo_h, 4)
    start_sides(borders)

    place = (dp, space, dp_count, space_count // 2)
    depth = 3 // PIECES
    assert depth == 1
    pieces = []
    for index in range(2 * PIECES):
        of, b0 = divmod(index, PIECES)
        bufs = groups[index * 9 : index * 9 + 9]
        pieces.append(Reduction(place, scale, b0, (*bufs, (out2, out1)[of]), sems[index * 12 : index * 12 + 12]))

    def grad_piece(index):
        of, b0 = divmod(index, PIECES)
        red = pieces[index]
        for step in range(depth):
            b = b0 * depth + step
            left, cat, first, count = ((at, ccat, 0, (strip + 2) * cols), (xt, hcat, cols, pixels))[of]
            kernel_grad(left, cat, first, count, b, red.full, red.half)
        red.start()

    share_dp = Exchange(
        dp_count,
        lambda k, to: make(
            esum, edp.at[dp if to else lax.rem(dp + dp_count - k, dp_count)], edp_s.at[k - 1], edp_r.at[k - 1],
            device_id=(lax.rem(dp + k, dp_count), space), device_id_type=MESH,
        ),
    )
    share_space = Exchange(
        space_count,
        lambda k, to: make(
            esp.at[space], esp.at[space if to else lax.rem(space + space_count - k, space_count)], esp_s.at[k - 1], esp_r.at[k - 1],
            device_id=(dp, lax.rem(space + k, space_count)), device_id_type=MESH,
        ),
    )

    def borders_in():
        wait_sides(borders)
        for side, p in ((0, 0), (1, strip + 1)):
            put(hcat, p * cols, jnp.where(inside[side], halo_h[side].astype(F32), 0.0), edge)
        esum[...] = jnp.zeros_like(esum)

    def embed_dp():
        edp[dp] = esum[...]
        share_dp.start()

    def embed_space():
        share_dp.wait_recv()
        value = edp[0]
        for k in range(1, dp_count):
            value = value + edp[k]
        esp[space] = value
        share_space.start()

    def embed_end():
        share_space.wait_recv()
        value = lax.fori_loop(1, space_count, lambda k, v: v + esp[k], esp[0])
        eout[...] = jnp.sum(value, axis=0, keepdims=True) * scale

    events = []
    tick = 3 // PIECES
    for index, red in enumerate(pieces):
        at_tick = index * tick
        events.append((at_tick, 1, functools.partial(grad_piece, index)))
        ready = at_tick + tick
        for delay, step in zip(DELAYS, (red.pair_to_dp, red.dp_to_outer, red.outer_to_gather, red.gather_dp, red.gather_pair)):
            events.append((ready + delay, 0, step))
    events.append((6, 2, borders_in))
    for i in range(strip // block):
        events.append((6 + i, 3, functools.partial(inputs, i)))
    finished = 6 + strip // block
    events += [(finished, 0, embed_dp), (finished + 4, 0, embed_space), (finished + 9, 0, embed_end)]
    for _, _, step in sorted(events, key=lambda event: event[:2]):
        step()
    end_sides(sides + borders)
    peaks.wait_send()
    share_dp.wait_send()
    share_space.wait_send()
    for red in pieces:
        red.finish()


def body(features, heights, cotangent, weight_first, weight_second, shade_embed):
    images, strip, cols, width = features.shape
    dp_count, space_count = lax.axis_size("dp"), lax.axis_size("space")
    total_rows = strip * space_count
    outer = space_count // 2
    scale = 1.0 / math.sqrt(images * dp_count * total_rows * cols)
    pixels = strip * cols
    halo = (strip + 2) * cols
    taps = 9 * width
    lanes = width // 2
    quarter = width // dp_count
    split = quarter % (16 * outer) == 0
    vmem = pltpu.VMEM
    dma = pltpu.SemaphoreType.DMA
    r3 = (outer - 1, 3, quarter // outer, lanes) if split else (outer, 3, quarter, lanes)
    reduction = [
        vmem((2, 3, width, lanes), F32), vmem((2, 3, width, lanes), BF16), vmem((3, width, lanes), BF16),
        vmem((3, quarter, lanes), F32), vmem((3, width, lanes), BF16), vmem((dp_count - 1, 3, quarter, lanes), BF16),
        vmem((3, quarter, lanes), F32), vmem((3, quarter, lanes), BF16), vmem(r3, BF16),
    ]
    pairs = [1, dp_count - 1, outer - 1, outer - 1, dp_count - 1, 1]
    phase_sems = [dma((count,)) for count in pairs for _ in range(2)]
    scratch = [
        vmem((8, cols), F32), vmem((space_count - 1, 8, cols), F32),
        vmem((2, cols, width), BF16), vmem((2, cols, width), BF16), vmem((2, cols, width), BF16), vmem((2, cols, width), BF16),
        vmem((128, cols), F32), vmem((pixels, 128), F32),
        vmem((halo, 3 * width), BF16), vmem((halo, 3 * width), BF16), vmem((halo, 3 * width), BF16),
        vmem((3 * width, pixels), BF16), vmem((3 * width, halo), BF16), vmem((pixels, width), F32),
        vmem((8, width), F32), vmem((dp_count, 8, width), F32), vmem((space_count, 8, width), F32),
        dma((6,)), dma((6,)), dma((space_count - 1,)), dma((space_count - 1,)),
        dma((dp_count - 1,)), dma((dp_count - 1,)), dma((space_count - 1,)), dma((space_count - 1,)),
        vmem((taps, width), BF16), vmem((taps, width), BF16), dma((2,)),
        *(reduction * (2 * PIECES)),
        *(phase_sems * (2 * PIECES)),
    ]
    spec = pl.BlockSpec(memory_space=pltpu.VMEM)
    gfeat, first, second, total = pl.pallas_call(
        functools.partial(kernel, (dp_count, space_count), scale, 2.0 / total_rows),
        out_shape=(
            jax.ShapeDtypeStruct((pixels, width), BF16),
            jax.ShapeDtypeStruct((3, 3, width, width), BF16),
            jax.ShapeDtypeStruct((3, 3, width, width), BF16),
            jax.ShapeDtypeStruct((1, width), F32),
        ),
        in_specs=[spec] * 3 + [pl.BlockSpec(memory_space=pl.ANY)] * 2 + [spec],
        out_specs=(spec,) * 4,
        scratch_shapes=scratch,
        compiler_params=pltpu.CompilerParams(collective_id=0, has_side_effects=True, vmem_limit_bytes=60 * 2**20),
        cost_estimate=pl.CostEstimate(flops=90 * pixels * width * width, bytes_accessed=2**24, transcendentals=pixels * width),
    )(
        features.reshape(pixels, width),
        heights.reshape(strip, cols),
        cotangent.reshape(pixels, width),
        weight_first.reshape(taps, width),
        weight_second.reshape(taps, width),
        shade_embed,
    )

    return gfeat.reshape(features.shape), first.astype(F32), second.astype(F32), total.reshape(width)


def solution(mesh):
    in_specs = (
        P("dp", "space", None, None),
        P("dp", "space", None),
        P("dp", "space", None, None),
        P(),
        P(),
        P(),
    )
    out_specs = (P("dp", "space", None, None), P(), P(), P())
    return jax.shard_map(body, mesh=mesh, in_specs=in_specs, out_specs=out_specs, check_vma=False)
```
